32 devices in a mesh: batch: 8 (over z, x), chan: 4 (over y, core).
Axes of the slice: x: 2, y: 2, z: 4, core: 2. Of those that a mesh axis runs over, the one named last changes fastest.
Arguments:
- images: bfloat16 [2048, 8, 8, 256], P('batch'), may hold values from -6 to 6
- picks: int32 [2048], P('batch'), may hold values from 0 to 255
- pairs: int32 [1024, 2], P('batch'), may hold values from 0 to 255
- w_one: float32 [2304, 512], P(None, 'chan'), may hold values from -0.125 to 0.125
- w_two: float32 [4608, 512], P(None, 'chan'), may hold values from -0.09375 to 0.09375
- w_proj: float32 [256, 512], P(None, 'chan'), may hold values from -0.375 to 0.375
- head: float32 [512, 10], P('chan'), may hold values from -1 to 1
- head_bias: float32 [10], replicated, may hold values from -3 to 3
- norm_params: float32 [6, 512], P(None, 'chan'), may hold values from -1.2 to 1.5, as said below
- m_one: float32 [2304, 512], P(None, 'chan'), may hold values from -1.0430813e-07 to 1.0430813e-07
- m_two: float32 [4608, 512], P(None, 'chan'), may hold values from -1.0430813e-07 to 1.0430813e-07
- m_proj: float32 [256, 512], P(None, 'chan'), may hold values from -1.0430813e-07 to 1.0430813e-07
- m_head: float32 [512, 10], P('chan'), may hold values from -9.1552734e-05 to 9.1552734e-05
- m_bias: float32 [10], replicated, may hold values from -0.00018310547 to 0.00018310547
- m_norm: float32 [6, 512], P(None, 'chan'), may hold values from -1.9073486e-05 to 1.9073486e-05
- v_one: float32 [2304, 512], P(None, 'chan'), may hold values from 2.3841858e-17 to 9.536743e-17
- v_two: float32 [4608, 512], P(None, 'chan'), may hold values from 2.3841858e-17 to 9.536743e-17
- v_proj: float32 [256, 512], P(None, 'chan'), may hold values from 2.3841858e-17 to 9.536743e-17
- v_head: float32 [512, 10], P('chan'), may hold values from 1.953125e-11 to 7.8125e-11
- v_bias: float32 [10], replicated, may hold values from 7.8125e-11 to 3.125e-10
- v_norm: float32 [6, 512], P(None, 'chan'), may hold values from 7.8125e-13 to 3.125e-12
Outputs:
- loss: float32 [1], replicated
- grad_norm: float32 [1], replicated
- new_one: float32 [2304, 512], P(None, 'chan')
- new_two: float32 [4608, 512], P(None, 'chan')
- new_proj: float32 [256, 512], P(None, 'chan')
- new_head: float32 [512, 10], P('chan')
- new_bias: float32 [10], replicated
- new_norm: float32 [6, 512], P(None, 'chan')
- next_m_one: float32 [2304, 512], P(None, 'chan')
- next_m_two: float32 [4608, 512], P(None, 'chan')
- next_m_proj: float32 [256, 512], P(None, 'chan')
- next_m_head: float32 [512, 10], P('chan')
- next_m_bias: float32 [10], replicated
- next_m_norm: float32 [6, 512], P(None, 'chan')
- next_v_one: float32 [2304, 512], P(None, 'chan')
- next_v_two: float32 [4608, 512], P(None, 'chan')
- next_v_proj: float32 [256, 512], P(None, 'chan')
- next_v_head: float32 [512, 10], P('chan')
- next_v_bias: float32 [10], replicated
- next_v_norm: float32 [6, 512], P(None, 'chan')
The draws below stay inside these ranges and needn't reach their ends.
Inputs may be any that keep to these rules, and one draw needn't show every extreme that they name: `picks`: each entry is a row of the images that the same index of batch holds. `pairs`: each entry is one of the 256 images run on the same index of batch. `norm_params`: rows 0, 2, 4 are gains, rows 1, 3, 5 shifts.
All inputs are finite; a program needn't handle non-finite values.
Results may differ from the reference program's by a relative error of at most 0.01.
The reference program's roundings to bfloat16 on the way count: a program that leaves them out, or rounds other values in their place, can miss the bound.
Values may be sent and summed in bfloat16 or wider, within the bound.
No kernel may reach another device: no remote copies, remote signals or barrier semaphores. Data moves between devices by JAX's collectives and lax.ppermute only.
A program may use at most 128 MiB of HBM per device.

```python
import math
from functools import partial
import jax
import jax.numpy as jnp
from jax import lax

CIN = 256
COUT = 512
NCLS = 10
STEPS = 10
B_DEV = 256
TAB_DEV = 256
PAIRS_DEV = 128
IMAGES = 2048
TABLE = 2048
PAIRS = 1024
N_BATCH = 8


def draw_norm_params(key, part):
    gain_key = jax.random.fold_in(key, 11)
    shift_key = jax.random.fold_in(key, 23)
    gains = jax.random.uniform(gain_key, (3, COUT), jnp.float32, 0.5, 1.5)
    shifts = jnp.clip(0.3 * jax.random.normal(shift_key, (3, COUT), jnp.float32), -1.2, 1.2)
    return jnp.stack([gains, shifts], axis=1).reshape(6, COUT)


def place_ends(entries, key, smallest, largest):
    longest = entries.shape.index(max(entries.shape))
    spots = []
    for shift in (0, 1):
        where = [jax.random.randint(jax.random.fold_in(key, axis), (), 0, length) for axis, length in enumerate(entries.shape)]
        where[longest] = (where[longest] + shift) % entries.shape[longest]
        spots.append(tuple(where))
    return entries.at[spots[0]].set(smallest).at[spots[1]].set(largest)


def block_scale(own_key, shape, cuts, smallest, largest):
    def one(dim, shards_of):
        steps = jax.random.uniform(jax.random.fold_in(jax.random.fold_in(own_key, 6), dim), (shards_of,), jnp.float32, smallest / len(cuts), largest / len(cuts))
        return jnp.repeat(jnp.exp(steps), shape[dim] // shards_of).reshape((-1,) + (1,) * (len(shape) - dim - 1))

    level = one(*cuts[0])
    for cut in cuts[1:]:
        level = level * one(*cut)
    return level


def normal_values(own_key, extent, scale, bound, cuts=(), kind=jnp.bfloat16):
    array = scale * jax.random.normal(own_key, extent, jnp.float32)
    if cuts:
        array = array * block_scale(own_key, extent, cuts, -0.22, 0.18)
    return jnp.clip(array, -bound, bound).astype(kind)


def setup_inputs(seed: int = 0) -> dict:
    streams_of = jax.random.split(jax.random.key(seed), 22)
    images = normal_values(streams_of[0], (TABLE, 8, 8, CIN), 1.0, 6.0, ((0, 8),))
    picks = place_ends(jax.random.randint(streams_of[1], (IMAGES,), 0, TAB_DEV), jax.random.fold_in(streams_of[1], 1), 0, TAB_DEV - 1).astype(jnp.int32)
    pairs = place_ends(jax.random.randint(streams_of[2], (PAIRS, 2), 0, B_DEV), jax.random.fold_in(streams_of[2], 1), 0, B_DEV - 1).astype(jnp.int32)
    w_one = normal_values(streams_of[3], (9 * CIN, COUT), (9 * CIN) ** -0.5, 0.125, ((1, 4),), jnp.float32)
    w_two = normal_values(streams_of[4], (9 * COUT, COUT), (9 * COUT) ** -0.5, 0.09375, ((1, 4),), jnp.float32)
    w_proj = normal_values(streams_of[5], (CIN, COUT), CIN ** -0.5, 0.375, ((1, 4),), jnp.float32)
    head = normal_values(streams_of[6], (COUT, NCLS), (COUT // 16) ** -0.5, 1.0, ((0, 4),), jnp.float32)
    head_bias = normal_values(streams_of[7], (NCLS,), 0.5, 3.0, (), jnp.float32)
    norm_params = draw_norm_params(jax.random.fold_in(streams_of[21], 71), 0)
    m_one = normal_values(streams_of[9], (9 * CIN, COUT), (0.000055 / (COUT * NCLS * IMAGES) ** 0.5), 1.043081283569336e-07, ((1, 4),), jnp.float32)
    m_two = normal_values(streams_of[10], (9 * COUT, COUT), (0.000055 / (COUT * NCLS * IMAGES) ** 0.5), 1.043081283569336e-07, ((1, 4),), jnp.float32)
    m_proj = normal_values(streams_of[11], (CIN, COUT), (0.000055 / (COUT * NCLS * IMAGES) ** 0.5), 1.043081283569336e-07, ((1, 4),), jnp.float32)
    m_head = normal_values(streams_of[12], (COUT, NCLS), (0.0011 / (COUT * NCLS) ** 0.5), 9.1552734375e-05, ((0, 4),), jnp.float32)
    m_bias = normal_values(streams_of[13], (NCLS,), (0.0022 / (COUT * NCLS) ** 0.5), 0.00018310547, (), jnp.float32)
    m_norm = normal_values(streams_of[14], (6, COUT), (0.00022 / (COUT * NCLS) ** 0.5), 1.9073486328125e-05, ((1, 4),), jnp.float32)
    v_one = jnp.clip(jnp.exp(math.log(9.536743291391677e-17) - 1.3862944 * jax.random.uniform(streams_of[15], (9 * CIN, COUT), jnp.float32) ** block_scale(streams_of[15], (9 * CIN, COUT), ((1, 4),), -0.2, 0.2)), 2.3841858228479194e-17, 9.536743291391677e-17)
    v_two = jnp.clip(jnp.exp(math.log(9.536743291391677e-17) - 1.3862944 * jax.random.uniform(streams_of[16], (9 * COUT, COUT), jnp.float32) ** block_scale(streams_of[16], (9 * COUT, COUT), ((1, 4),), -0.2, 0.2)), 2.3841858228479194e-17, 9.536743291391677e-17)
    v_proj = jnp.clip(jnp.exp(math.log(9.536743291391677e-17) - 1.3862944 * jax.random.uniform(streams_of[17], (CIN, COUT), jnp.float32) ** block_scale(streams_of[17], (CIN, COUT), ((1, 4),), -0.2, 0.2)), 2.3841858228479194e-17, 9.536743291391677e-17)
    v_head = jnp.clip(jnp.exp(math.log(7.812499952519758e-11) - 1.3862944 * jax.random.uniform(streams_of[18], (COUT, NCLS), jnp.float32) ** block_scale(streams_of[18], (COUT, NCLS), ((0, 4),), -0.2, 0.2)), 1.9531249881299395e-11, 7.812499952519758e-11)
    v_bias = jnp.clip(jnp.exp(jax.random.uniform(streams_of[19], (NCLS,), jnp.float32, math.log(7.812499952519758e-11), math.log(3.124999981007903e-10))), 7.812499952519758e-11, 3.124999981007903e-10)
    v_norm = jnp.clip(jnp.exp(math.log(3.125000041723225e-12) - 1.3862944 * jax.random.uniform(streams_of[20], (6, COUT), jnp.float32) ** block_scale(streams_of[20], (6, COUT), ((1, 4),), -0.2, 0.2)), 7.812500104308062e-13, 3.125000041723225e-12)
    return {"images": images, "picks": picks, "pairs": pairs, "w_one": w_one, "w_two": w_two, "w_proj": w_proj, "head": head, "head_bias": head_bias, "norm_params": norm_params, "m_one": m_one, "m_two": m_two, "m_proj": m_proj, "m_head": m_head, "m_bias": m_bias, "m_norm": m_norm, "v_one": v_one, "v_two": v_two, "v_proj": v_proj, "v_head": v_head, "v_bias": v_bias, "v_norm": v_norm}


@jax.custom_vjp
def low(v):
    return lax.optimization_barrier(v.astype(jnp.bfloat16)).astype(jnp.float32)

@jax.custom_vjp
def low_back(v):
    return v

def low_keep(v):
    return (low(v), None)

def low_pass(kept, grad):
    return (grad,)

def back_keep(v):
    return (v, None)

def back_low(kept, grad):
    return (low(grad),)
low.defvjp(low_keep, low_pass)
low_back.defvjp(back_keep, back_low)
NORM_EPS = 1e-05
ENTROPY_WEIGHT = 5.0
CLIP_LIMIT = 0.01
LEARN_RATE = 0.15
BETA_FIRST = 0.9
BETA_SECOND = 0.999
ADAM_EPS = 1e-08
WEIGHT_DECAY = 0.01
HIGHEST = lax.Precision.HIGHEST

def convolve(inputs, weight, stride):
    kernel = weight.reshape(3, 3, weight.shape[0] // 9, weight.shape[1])
    return lax.conv_general_dilated(inputs, kernel, (stride, stride), ((1, 1), (1, 1)), dimension_numbers=('NHWC', 'HWIO', 'NHWC'), precision=HIGHEST)

def batch_norm(values, gain, shift):
    average = lax.optimization_barrier(jnp.mean(values, axis=(0, 1, 2)))
    spread = lax.optimization_barrier(jnp.mean(values * values, axis=(0, 1, 2))) - average * average
    return (values - average) * lax.rsqrt(spread + NORM_EPS) * gain + shift

def forward(w_one, w_two, w_proj, head, head_bias, norm_params, inputs, first_index, second_index):
    conv_one = low_back(convolve(inputs, low(w_one), 2))
    hidden = low(jax.nn.silu(batch_norm(conv_one, norm_params[0], norm_params[1])))
    conv_two = low_back(convolve(hidden, low(w_two), 1))
    shortcut = low_back(jnp.einsum('bhwc,ck->bhwk', inputs[:, ::2, ::2, :], low(w_proj), precision=HIGHEST))
    joined = jax.nn.silu(batch_norm(conv_two, norm_params[2], norm_params[3]) + batch_norm(shortcut, norm_params[4], norm_params[5]))
    pooled = low(lax.optimization_barrier(jnp.mean(joined, axis=(1, 2))))
    logits = low_back(jnp.dot(pooled, low(head), precision=HIGHEST)) + head_bias
    probs = jax.nn.softmax(logits, axis=1)
    similar = lax.optimization_barrier(jnp.sum(probs[first_index] * probs[second_index], axis=1))
    mass = lax.optimization_barrier(jnp.mean(probs, axis=0))
    return -jnp.mean(jnp.log(similar)) + ENTROPY_WEIGHT * jnp.sum(mass * jnp.log(mass))

def pick_rows(table_rows, indices):
    return table_rows[indices]

def adam(weight, gradient, first, second, bias_one, bias_two, decay):
    first_new = BETA_FIRST * first + (1.0 - BETA_FIRST) * gradient
    second_new = BETA_SECOND * second + (1.0 - BETA_SECOND) * gradient * gradient
    stepped = first_new / bias_one / (jnp.sqrt(second_new / bias_two) + ADAM_EPS)
    return (weight - LEARN_RATE * (stepped + decay * weight), first_new, second_new)

def reference(images, picks, pairs, w_one, w_two, w_proj, head, head_bias, norm_params, m_one, m_two, m_proj, m_head, m_bias, m_norm, v_one, v_two, v_proj, v_head, v_bias, v_norm):
    table = images.reshape(N_BATCH, TAB_DEV, 8, 8, CIN)
    chosen = picks.reshape(N_BATCH, B_DEV)
    inputs = jax.vmap(pick_rows)(table, chosen).reshape(IMAGES, 8, 8, CIN).astype(jnp.float32)
    offsets = (jnp.arange(PAIRS) // PAIRS_DEV * B_DEV).astype(jnp.int32)
    first_index = pairs[:, 0].astype(jnp.int32) + offsets
    second_index = pairs[:, 1].astype(jnp.int32) + offsets
    weights = (w_one, w_two, w_proj, head, head_bias, norm_params)
    loss, pull = jax.vjp(partial(forward, inputs=inputs, first_index=first_index, second_index=second_index), *weights)
    grads = pull(jnp.ones_like(loss))
    squared = sum((jnp.sum(gradient * gradient) for gradient in grads))
    grad_norm = jnp.sqrt(squared)
    scale = jnp.minimum(1.0, CLIP_LIMIT / (grad_norm + 1e-06))
    step = jnp.float32(STEPS)
    bias_one = 1.0 - jnp.power(jnp.float32(BETA_FIRST), step)
    bias_two = 1.0 - jnp.power(jnp.float32(BETA_SECOND), step)
    firsts = (m_one, m_two, m_proj, m_head, m_bias, m_norm)
    seconds = (v_one, v_two, v_proj, v_head, v_bias, v_norm)
    decays = (WEIGHT_DECAY, WEIGHT_DECAY, WEIGHT_DECAY, WEIGHT_DECAY, 0.0, 0.0)
    results = [adam(weight, gradient * scale, first, second, bias_one, bias_two, decay) for weight, gradient, first, second, decay in zip(weights, grads, firsts, seconds, decays)]
    return (loss.reshape(1), grad_norm.reshape(1), results[0][0], results[1][0], results[2][0], results[3][0], results[4][0], results[5][0], results[0][1], results[1][1], results[2][1], results[3][1], results[4][1], results[5][1], results[0][2], results[1][2], results[2][2], results[3][2], results[4][2], results[5][2])
```

```python
import math

import jax
import jax.numpy as jnp
from jax import lax
from jax.sharding import PartitionSpec as P

STEPS = 10


NORM_EPS = 1e-05
ENTROPY_WEIGHT = 5.0
CLIP_LIMIT = 0.01
LEARN_RATE = 0.15
BETA_FIRST = 0.9
BETA_SECOND = 0.999
ADAM_EPS = 1e-08
WEIGHT_DECAY = 0.01
MAPS = ("HWNC", "HWIO", "HWNC")
BF16 = jnp.bfloat16
F32 = jnp.float32
HIGHEST = lax.Precision.HIGHEST


def swap(values, axis, bit):
    count = lax.axis_size(axis)
    return lax.ppermute(values, axis, [(i, i ^ bit) for i in range(count)])


def in_order(bit, own, other, axis):
    first = jnp.where(bit == 0, own, other)
    second = jnp.where(bit == 0, other, own)
    return jnp.concatenate([first, second], axis=axis)


def sum_images(values):
    values = values + swap(values, "chan", 1)
    groups = lax.axis_size("batch")
    spread = jnp.broadcast_to(values[None], (groups,) + values.shape)
    return jnp.sum(lax.all_to_all(spread, "batch", 0, 0), axis=0)


def batch_bits():
    bits = []
    bit = 1
    while bit < lax.axis_size("batch"):
        bits.append(bit)
        bit *= 2
    return bits


def scatter_step(part, bit):
    rows = part.shape[0] // 2
    mine = (lax.axis_index("batch") // bit) % 2
    keep = lax.dynamic_slice_in_dim(part, mine * rows, rows, 0)
    give = lax.dynamic_slice_in_dim(part, (1 - mine) * rows, rows, 0)
    got = swap(give.astype(BF16), "batch", bit)
    return keep + got.astype(F32)


def gather_step(part, bit):
    mine = (lax.axis_index("batch") // bit) % 2
    got = swap(part, "batch", bit)
    return in_order(mine, part, got, 0)


def conv(maps, weight, stride):
    kernel = weight.reshape(3, 3, weight.shape[0] // 9, weight.shape[1])
    return lax.conv_general_dilated(
        maps,
        kernel,
        (stride, stride),
        ((1, 1), (1, 1)),
        dimension_numbers=MAPS,
        preferred_element_type=F32,
    )


def conv_back(grads, weight):
    kernel = weight.reshape((3, 3) + weight.shape[1:])[::-1, ::-1]
    return lax.conv_general_dilated(
        grads,
        kernel,
        (1, 1),
        ((1, 1), (1, 1)),
        dimension_numbers=("HWNC", "HWOI", "HWNC"),
        preferred_element_type=F32,
    )


def weight_grad(maps, grads, stride):
    result = lax.conv_general_dilated(
        maps,
        grads,
        (1, 1),
        ((1, 2 - stride), (1, 2 - stride)),
        rhs_dilation=(stride, stride),
        dimension_numbers=("HWCN", "HWIO", "HWNC"),
        preferred_element_type=F32,
    )
    return result.reshape(9 * maps.shape[3], grads.shape[3])


def likely_mean(gain_shift):
    gain, shift = gain_shift[0], gain_shift[1]
    spread = math.sqrt(3.0) * gain
    ends = jax.nn.silu(shift + spread) + jax.nn.silu(shift - spread)
    return (4.0 * jax.nn.silu(shift) + ends) / 6.0


def outer_taps(centre, tap_sums):
    return (centre[None, :, None] * tap_sums[:, None, :]).reshape(-1, tap_sums.shape[1])


def channel_sums(values):
    return jnp.sum(values, axis=(0, 1, 2))


def silu_slope(values):
    sigma = jax.nn.sigmoid(values)
    return sigma * (1.0 + values * (1.0 - sigma))


def normalize(values, total, squares, count, gain, shift):
    average = total / count
    spread = squares / count - average * average
    scale = lax.rsqrt(spread + NORM_EPS)
    centred = (values - average) * scale
    return (centred, scale, centred * gain + shift)


def norm_back(grads, centred, scale, gain, sum_grad, sum_cross, count):
    return scale * gain * (grads - sum_grad / count - centred * sum_cross / count)


def adam(weight, gradient, first, second, bias_one, bias_two, decay):
    first_new = BETA_FIRST * first + (1.0 - BETA_FIRST) * gradient
    second_new = BETA_SECOND * second + (1.0 - BETA_SECOND) * gradient * gradient
    stepped = first_new / bias_one / (jnp.sqrt(second_new / bias_two) + ADAM_EPS)
    return (weight - LEARN_RATE * (stepped + decay * weight), first_new, second_new)


def per_device(
    images,
    picks,
    pairs,
    w_one,
    w_two,
    w_proj,
    head,
    head_bias,
    norm_params,
    m_one,
    m_two,
    m_proj,
    m_head,
    m_bias,
    m_norm,
    v_one,
    v_two,
    v_proj,
    v_head,
    v_bias,
    v_norm,
):
    groups = lax.axis_size("batch")
    images_all = picks.shape[0] * groups
    pixels = images_all * 16.0
    pairs_all = pairs.shape[0] * groups
    width = w_one.shape[1]
    classes = head.shape[1]
    chan = lax.axis_index("chan")
    low, high = chan % 2, chan // 2
    count = picks.shape[0] // 2

    one_bf, two_bf, proj_bf = (w.astype(BF16) for w in (w_one, w_two, w_proj))
    one_full = in_order(low, one_bf, swap(one_bf, "chan", 1), 1)
    small = jnp.concatenate([norm_params, head.T], axis=0)
    small = in_order(low, small, swap(small, "chan", 1), 1)
    params = small[:6]
    params_other = swap(params[:2], "chan", 2)
    head_t = small[6:].astype(BF16)
    proj_full = in_order(low, proj_bf, swap(proj_bf, "chan", 1), 1)
    two_full = in_order(low, two_bf, swap(two_bf, "chan", 1), 1)
    two_full = two_full.reshape(9, 2, 2 * width, 2 * width)
    two_own = lax.dynamic_index_in_dim(two_full, high, 1, False)
    two_other = lax.dynamic_index_in_dim(two_full, 1 - high, 1, False)

    mine = lax.dynamic_slice_in_dim(picks, low * count, count, 0)
    inputs = images[mine].transpose(1, 2, 0, 3)
    strided = inputs[::2, ::2]
    conv_one = conv(inputs, one_full, 2)
    shortcut = jnp.einsum("hwbc,ck->hwbk", strided, proj_full, preferred_element_type=F32)
    sums = sum_images(
        jnp.stack(
            [
                channel_sums(conv_one),
                channel_sums(conv_one * conv_one),
                channel_sums(shortcut),
                channel_sums(shortcut * shortcut),
            ]
        )
    )
    centred_one, scale_one, normed_one = normalize(
        conv_one, sums[0], sums[1], pixels, params[0], params[1]
    )
    centred_short, scale_short, normed_short = normalize(
        shortcut, sums[2], sums[3], pixels, params[4], params[5]
    )
    hidden = jax.nn.silu(normed_one).astype(BF16)
    hidden_other = swap(hidden, "chan", 2)
    conv_two = conv(hidden, two_own.reshape(-1, 2 * width), 1)
    conv_two = conv_two + conv(hidden_other, two_other.reshape(-1, 2 * width), 1)
    sums = sum_images(jnp.stack([channel_sums(conv_two), channel_sums(conv_two * conv_two)]))
    centred_two, scale_two, normed_two = normalize(
        conv_two, sums[0], sums[1], pixels, params[2], params[3]
    )
    summed = normed_two + normed_short
    joined = jax.nn.silu(summed)
    slope = silu_slope(summed)
    pooled = (jnp.sum(joined, axis=(0, 1)) / 16.0).astype(BF16)
    slope_sums = jnp.stack(
        [
            jnp.sum(slope, axis=(0, 1)),
            jnp.sum(slope * centred_two, axis=(0, 1)),
            jnp.sum(slope * centred_short, axis=(0, 1)),
        ]
    ) / 16.0

    logits_part = jnp.einsum("bc,kc->bk", pooled, head_t, preferred_element_type=F32)
    logits_part = in_order(low, logits_part, swap(logits_part, "chan", 1), 0)
    logits = logits_part + swap(logits_part, "chan", 2) + head_bias
    probs_all = jax.nn.softmax(logits, axis=1)
    probs = lax.dynamic_slice_in_dim(probs_all, low * count, count, 0)
    ids = jnp.arange(2 * count, dtype=pairs.dtype)
    hot_a = (pairs[:, :1] == ids).astype(F32)
    hot_b = (pairs[:, 1:] == ids).astype(F32)
    probs_a = jnp.dot(hot_a, probs_all, precision=HIGHEST)
    probs_b = jnp.dot(hot_b, probs_all, precision=HIGHEST)
    similar = jnp.sum(probs_a * probs_b, axis=1, keepdims=True)
    pull = jnp.einsum("pb,pk->bk", hot_a, probs_b / similar, precision=HIGHEST)
    pull = pull + jnp.einsum("pb,pk->bk", hot_b, probs_a / similar, precision=HIGHEST)
    pull = lax.dynamic_slice_in_dim(pull, low * count, count, 0)
    dprobs = -pull / pairs_all
    dlogits_pair = probs * (dprobs - jnp.sum(probs * dprobs, axis=1, keepdims=True))

    head_f = lax.optimization_barrier(head_t.astype(F32))
    dpooled_pair = jnp.dot(dlogits_pair, head_f, precision=HIGHEST)
    mixed = jnp.dot(probs, head_f, precision=HIGHEST)
    pair_rows = jnp.sum(slope_sums * dpooled_pair, axis=1)
    mass_rows = head_f[:, None] * jnp.einsum("bj,sbc->jsc", probs, slope_sums, precision=HIGHEST)
    mass_rows = mass_rows - jnp.einsum("bj,sbc->jsc", probs, slope_sums * mixed, precision=HIGHEST)
    gram = jnp.einsum("bj,bk->jk", probs, probs, precision=HIGHEST)
    scalars = jnp.concatenate(
        [
            gram.reshape(-1),
            jnp.sum(probs, axis=0),
            jnp.sum(dlogits_pair, axis=0),
            0.5 * jnp.sum(jnp.log(similar))[None],
        ]
    )
    scalars = jnp.pad(scalars, (0, 2 * width - scalars.shape[0]))
    sums = sum_images(
        jnp.concatenate(
            [pair_rows, mass_rows.reshape(3 * classes, -1), scalars[None]], axis=0
        )
    )
    scalars = sums[3 + 3 * classes]
    gram = scalars[: classes * classes].reshape(classes, classes)
    mass_total = scalars[classes * classes : classes * (classes + 1)]
    mass = mass_total / images_all
    pull_mass = ENTROPY_WEIGHT * (jnp.log(mass) + 1.0) / images_all
    pair_total = scalars[classes * (classes + 2)]
    loss = -pair_total / pairs_all + ENTROPY_WEIGHT * jnp.sum(mass * jnp.log(mass))
    grad_bias = (
        scalars[classes * (classes + 1) : classes * (classes + 2)]
        + pull_mass * mass_total
        - jnp.sum(gram * pull_mass[:, None], axis=0)
    )
    upper = sums[:3] + jnp.sum(
        pull_mass[:, None, None] * sums[3 : 3 + 3 * classes].reshape(classes, 3, -1), axis=0
    )
    sum_top, cross_two, cross_short = upper[0], upper[1], upper[2]
    dlogits = dlogits_pair + probs * (
        pull_mass - jnp.sum(probs * pull_mass, axis=1, keepdims=True)
    )
    dlogits_bf = dlogits.astype(BF16)
    grad_head = jnp.einsum("bk,bc->kc", dlogits_bf, pooled, preferred_element_type=F32)
    dpooled = jnp.dot(dlogits, head_f, precision=HIGHEST)
    djoined = (dpooled / 16.0) * slope
    dconv_two = norm_back(
        djoined, centred_two, scale_two, params[2], sum_top, cross_two, pixels
    ).astype(BF16)
    dshort = norm_back(
        djoined, centred_short, scale_short, params[4], sum_top, cross_short, pixels
    ).astype(BF16)

    dhidden_other = conv_back(dconv_two, two_other).astype(BF16)
    dhidden_got = swap(dhidden_other, "chan", 2)
    dhidden = conv_back(dconv_two, two_own)

    def channel_half(full):
        keep = lax.dynamic_slice_in_dim(full, low * width, width, 1)
        give = lax.dynamic_slice_in_dim(full, (1 - low) * width, width, 1)
        return keep + swap(give.astype(BF16), "chan", 1).astype(F32)

    centre = in_order(high, likely_mean(params[:2]), likely_mean(params_other), 0)
    pixel_sums = jnp.sum(dconv_two.astype(F32), axis=2)
    tap_sums = jnp.stack(
        [
            jnp.sum(pixel_sums[max(0, 1 - i) : 5 - i, max(0, 1 - j) : 5 - j], axis=(0, 1))
            for i in range(3)
            for j in range(3)
        ]
    )
    own = weight_grad(hidden, dconv_two, 1).reshape(9, 1, 2 * width, -1)
    other = weight_grad(hidden_other, dconv_two, 1).reshape(9, 1, 2 * width, -1)
    grad_two = in_order(high, own, other, 1).reshape(-1, 2 * width)
    grad_proj = jnp.einsum("hwbc,hwbk->ck", strided, dshort, preferred_element_type=F32)
    grad_two = grad_two - outer_taps(centre, tap_sums)
    grad_upper = channel_half(jnp.concatenate([grad_two, grad_proj], axis=0))

    dhidden = dhidden + dhidden_got.astype(F32)
    dnormed_one = dhidden * silu_slope(normed_one)
    sums = sum_images(
        jnp.concatenate(
            [
                jnp.stack([channel_sums(dnormed_one), channel_sums(dnormed_one * centred_one)]),
                grad_head,
                tap_sums,
            ],
            axis=0,
        )
    )
    sum_low, cross_low = sums[0], sums[1]
    grad_head = lax.dynamic_slice_in_dim(sums[2 : 2 + classes], low * width, width, 1).T
    tap_sums = lax.dynamic_slice_in_dim(sums[2 + classes :], low * width, width, 1)
    missing = outer_taps(centre, tap_sums)
    missing = jnp.concatenate([missing, jnp.zeros(w_proj.shape, F32)], axis=0)
    dconv_one = norm_back(
        dnormed_one, centred_one, scale_one, params[0], sum_low, cross_low, pixels
    ).astype(BF16)
    grad_lower = channel_half(weight_grad(inputs, dconv_one, 2))

    bits = batch_bits()
    shifted = bits[1:] + bits[:1]
    orders = (bits, shifted)

    def halves(values):
        rows = values.shape[0] // 2
        return [values[:rows], values[rows:]]

    upper_parts = halves(grad_upper)
    lower_parts = halves(grad_lower)
    parts = upper_parts + lower_parts
    parts = [
        _scatter(part, orders[index % 2]) for index, part in enumerate(parts)
    ]
    for index, rest in enumerate(halves(missing)):
        parts[index] = parts[index] + _own_rows(rest, orders[index % 2])
    squares = sum(jnp.sum(part * part) for part in parts)
    parts = [part.astype(BF16) for part in parts]
    parts = [_gather(part, orders[index % 2]) for index, part in enumerate(parts)]
    grad_upper = jnp.concatenate(parts[:2], axis=0).astype(F32)
    grad_one = jnp.concatenate(parts[2:], axis=0).astype(F32)
    grad_two, grad_proj = grad_upper[: w_two.shape[0]], grad_upper[w_two.shape[0] :]

    grad_norm_params = jnp.stack(
        [cross_low, sum_low, cross_two, sum_top, cross_short, sum_top], axis=0
    )
    grad_norm_params = lax.dynamic_slice_in_dim(grad_norm_params, low * width, width, 1)
    replicated = jnp.sum(grad_norm_params * grad_norm_params) + jnp.sum(grad_head * grad_head)
    replicated = replicated + jnp.sum(grad_bias * grad_bias) / lax.axis_size("chan")
    squares = jnp.broadcast_to(squares + replicated / groups, (8, 128))
    bit = 1
    while bit < lax.axis_size("chan"):
        squares = squares + swap(squares, "chan", bit)
        bit *= 2
    for bit in bits:
        squares = squares + swap(squares, "batch", bit)
    grad_norm = jnp.sqrt(squares[0, 0])
    scale = jnp.minimum(1.0, CLIP_LIMIT / (grad_norm + 1e-06))
    step = jnp.float32(STEPS)
    bias_one = 1.0 - jnp.power(jnp.float32(BETA_FIRST), step)
    bias_two = 1.0 - jnp.power(jnp.float32(BETA_SECOND), step)
    grads = (grad_one, grad_two, grad_proj, grad_head, grad_bias, grad_norm_params)
    weights = (w_one, w_two, w_proj, head, head_bias, norm_params)
    firsts = (m_one, m_two, m_proj, m_head, m_bias, m_norm)
    seconds = (v_one, v_two, v_proj, v_head, v_bias, v_norm)
    decays = (WEIGHT_DECAY, WEIGHT_DECAY, WEIGHT_DECAY, WEIGHT_DECAY, 0.0, 0.0)
    results = [
        adam(weight, gradient * scale, first, second, bias_one, bias_two, decay)
        for weight, gradient, first, second, decay in zip(weights, grads, firsts, seconds, decays)
    ]
    return (
        loss.reshape(1),
        grad_norm.reshape(1),
        *(result[0] for result in results),
        *(result[1] for result in results),
        *(result[2] for result in results),
    )


def _scatter(part, order):
    for bit in order:
        part = scatter_step(part, bit)
    return part


def _own_rows(full, order):
    rows, start = full.shape[0], 0
    for bit in order:
        rows //= 2
        start = start + (lax.axis_index("batch") // bit) % 2 * rows
    return lax.dynamic_slice_in_dim(full, start, rows, 0)


def _gather(part, order):
    for bit in reversed(order):
        part = gather_step(part, bit)
    return part


def solution(mesh):
    placed = (
        P("batch", None, None, None),
        P("batch"),
        P("batch", None),
        P(None, "chan"),
        P(None, "chan"),
        P(None, "chan"),
        P("chan", None),
        P(),
        P(None, "chan"),
        P(None, "chan"),
        P(None, "chan"),
        P(None, "chan"),
        P("chan", None),
        P(),
        P(None, "chan"),
        P(None, "chan"),
        P(None, "chan"),
        P(None, "chan"),
        P("chan", None),
        P(),
        P(None, "chan"),
    )
    return jax.shard_map(
        per_device,
        mesh=mesh,
        in_specs=placed,
        out_specs=(
            P(),
            P(),
            P(None, "chan"),
            P(None, "chan"),
            P(None, "chan"),
            P("chan", None),
            P(),
            P(None, "chan"),
            P(None, "chan"),
            P(None, "chan"),
            P(None, "chan"),
            P("chan", None),
            P(),
            P(None, "chan"),
            P(None, "chan"),
            P(None, "chan"),
            P(None, "chan"),
            P("chan", None),
            P(),
            P(None, "chan"),
        ),
        check_vma=False,
    )
```

```python
import math

import jax
import jax.numpy as jnp
from jax import lax
from jax.sharding import PartitionSpec as P

STEPS = 10


NORM_EPS = 1e-05
ENTROPY_WEIGHT = 5.0
CLIP_LIMIT = 0.01
LEARN_RATE = 0.15
BETA_FIRST = 0.9
BETA_SECOND = 0.999
ADAM_EPS = 1e-08
WEIGHT_DECAY = 0.01
MAPS = ("HWNC", "HWIO", "HWNC")
BF16 = jnp.bfloat16
F32 = jnp.float32
HIGHEST = lax.Precision.HIGHEST


def swap(values, axis, bit):
    count = lax.axis_size(axis)
    return lax.ppermute(values, axis, [(i, i ^ bit) for i in range(count)])


def in_order(bit, own, other, axis):
    first = jnp.where(bit == 0, own, other)
    second = jnp.where(bit == 0, other, own)
    return jnp.concatenate([first, second], axis=axis)


def sum_images(values):
    values = values + swap(values, "chan", 1)
    groups = lax.axis_size("batch")
    spread = jnp.broadcast_to(values[None], (groups,) + values.shape)
    return jnp.sum(lax.all_to_all(spread, "batch", 0, 0), axis=0)


def after(values, *others):
    return lax.optimization_barrier((values,) + others)[0]


def batch_bits():
    bits = []
    bit = 1
    while bit < lax.axis_size("batch"):
        bits.append(bit)
        bit *= 2
    return bits


def scatter_step(part, bit):
    rows = part.shape[0] // 2
    mine = (lax.axis_index("batch") // bit) % 2
    keep = lax.dynamic_slice_in_dim(part, mine * rows, rows, 0)
    give = lax.dynamic_slice_in_dim(part, (1 - mine) * rows, rows, 0)
    got = swap(give.astype(BF16), "batch", bit)
    return keep + got.astype(F32)


def gather_step(part, bit):
    mine = (lax.axis_index("batch") // bit) % 2
    got = swap(part, "batch", bit)
    return in_order(mine, part, got, 0)


def conv(maps, weight, stride):
    kernel = weight.reshape(3, 3, weight.shape[0] // 9, weight.shape[1])
    return lax.conv_general_dilated(
        maps,
        kernel,
        (stride, stride),
        ((1, 1), (1, 1)),
        dimension_numbers=MAPS,
        preferred_element_type=F32,
    )


def conv_back(grads, weight):
    kernel = weight.reshape((3, 3) + weight.shape[1:])[::-1, ::-1]
    return lax.conv_general_dilated(
        grads,
        kernel,
        (1, 1),
        ((1, 1), (1, 1)),
        dimension_numbers=("HWNC", "HWOI", "HWNC"),
        preferred_element_type=F32,
    )


def weight_grad(maps, grads, stride):
    result = lax.conv_general_dilated(
        maps,
        grads,
        (1, 1),
        ((1, 2 - stride), (1, 2 - stride)),
        rhs_dilation=(stride, stride),
        dimension_numbers=("HWCN", "HWIO", "HWNC"),
        preferred_element_type=F32,
    )
    return result.reshape(9 * maps.shape[3], grads.shape[3])


def likely_mean(gain_shift):
    gain, shift = gain_shift[0], gain_shift[1]
    spread = math.sqrt(3.0) * gain
    ends = jax.nn.silu(shift + spread) + jax.nn.silu(shift - spread)
    return (4.0 * jax.nn.silu(shift) + ends) / 6.0


def outer_taps(centre, tap_sums):
    return (centre[None, :, None] * tap_sums[:, None, :]).reshape(-1, tap_sums.shape[1])


def channel_sums(values):
    return jnp.sum(values, axis=(0, 1, 2))


def silu_slope(values):
    sigma = jax.nn.sigmoid(values)
    return sigma * (1.0 + values * (1.0 - sigma))


def normalize(values, total, squares, count, gain, shift):
    average = total / count
    spread = squares / count - average * average
    scale = lax.rsqrt(spread + NORM_EPS)
    centred = (values - average) * scale
    return (centred, scale, centred * gain + shift)


def norm_back(grads, centred, scale, gain, sum_grad, sum_cross, count):
    return scale * gain * (grads - sum_grad / count - centred * sum_cross / count)


def adam(weight, gradient, first, second, bias_one, bias_two, decay):
    first_new = BETA_FIRST * first + (1.0 - BETA_FIRST) * gradient
    second_new = BETA_SECOND * second + (1.0 - BETA_SECOND) * gradient * gradient
    stepped = first_new / bias_one / (jnp.sqrt(second_new / bias_two) + ADAM_EPS)
    return (weight - LEARN_RATE * (stepped + decay * weight), first_new, second_new)


def per_device(
    images,
    picks,
    pairs,
    w_one,
    w_two,
    w_proj,
    head,
    head_bias,
    norm_params,
    m_one,
    m_two,
    m_proj,
    m_head,
    m_bias,
    m_norm,
    v_one,
    v_two,
    v_proj,
    v_head,
    v_bias,
    v_norm,
):
    groups = lax.axis_size("batch")
    images_all = picks.shape[0] * groups
    pixels = images_all * 16.0
    pairs_all = pairs.shape[0] * groups
    width = w_one.shape[1]
    classes = head.shape[1]
    chan = lax.axis_index("chan")
    low, high = chan % 2, chan // 2
    count = picks.shape[0] // 2

    one_bf, two_bf, proj_bf = (w.astype(BF16) for w in (w_one, w_two, w_proj))
    one_full = in_order(low, one_bf, swap(one_bf, "chan", 1), 1)
    small = jnp.concatenate([norm_params, head.T], axis=0)
    small = in_order(low, small, swap(small, "chan", 1), 1)
    params = small[:6]
    params_other = swap(params[:2], "chan", 2)
    head_t = small[6:].astype(BF16)
    proj_full = in_order(low, proj_bf, swap(proj_bf, "chan", 1), 1)
    two_full = in_order(low, two_bf, swap(two_bf, "chan", 1), 1)
    two_full = two_full.reshape(9, 2, 2 * width, 2 * width)
    two_own = lax.dynamic_index_in_dim(two_full, high, 1, False)
    two_other = lax.dynamic_index_in_dim(two_full, 1 - high, 1, False)

    mine = lax.dynamic_slice_in_dim(picks, low * count, count, 0)
    inputs = images[mine].transpose(1, 2, 0, 3)
    strided = inputs[::2, ::2]
    conv_one = conv(inputs, one_full, 2)
    shortcut = jnp.einsum("hwbc,ck->hwbk", strided, proj_full, preferred_element_type=F32)
    sums = sum_images(
        jnp.stack(
            [
                channel_sums(conv_one),
                channel_sums(conv_one * conv_one),
                channel_sums(shortcut),
                channel_sums(shortcut * shortcut),
            ]
        )
    )
    centred_one, scale_one, normed_one = normalize(
        conv_one, sums[0], sums[1], pixels, params[0], params[1]
    )
    centred_short, scale_short, normed_short = normalize(
        shortcut, sums[2], sums[3], pixels, params[4], params[5]
    )
    hidden = jax.nn.silu(normed_one).astype(BF16)
    hidden_other = swap(hidden, "chan", 2)
    conv_two = conv(hidden, two_own.reshape(-1, 2 * width), 1)
    conv_two = conv_two + conv(hidden_other, two_other.reshape(-1, 2 * width), 1)
    sums = sum_images(jnp.stack([channel_sums(conv_two), channel_sums(conv_two * conv_two)]))
    centred_two, scale_two, normed_two = normalize(
        conv_two, sums[0], sums[1], pixels, params[2], params[3]
    )
    summed = normed_two + normed_short
    joined = jax.nn.silu(summed)
    slope = silu_slope(summed)
    pooled = (jnp.sum(joined, axis=(0, 1)) / 16.0).astype(BF16)
    slope_sums = jnp.stack(
        [
            jnp.sum(slope, axis=(0, 1)),
            jnp.sum(slope * centred_two, axis=(0, 1)),
            jnp.sum(slope * centred_short, axis=(0, 1)),
        ]
    ) / 16.0

    logits_part = jnp.einsum("bc,kc->bk", pooled, head_t, preferred_element_type=F32)
    logits_part = in_order(low, logits_part, swap(logits_part, "chan", 1), 0)
    logits = logits_part + swap(logits_part, "chan", 2) + head_bias
    probs_all = jax.nn.softmax(logits, axis=1)
    probs = lax.dynamic_slice_in_dim(probs_all, low * count, count, 0)
    ids = jnp.arange(2 * count, dtype=pairs.dtype)
    hot_a = (pairs[:, :1] == ids).astype(F32)
    hot_b = (pairs[:, 1:] == ids).astype(F32)
    probs_a = jnp.dot(hot_a, probs_all, precision=HIGHEST)
    probs_b = jnp.dot(hot_b, probs_all, precision=HIGHEST)
    similar = jnp.sum(probs_a * probs_b, axis=1, keepdims=True)
    pull = jnp.einsum("pb,pk->bk", hot_a, probs_b / similar, precision=HIGHEST)
    pull = pull + jnp.einsum("pb,pk->bk", hot_b, probs_a / similar, precision=HIGHEST)
    pull = lax.dynamic_slice_in_dim(pull, low * count, count, 0)
    dprobs = -pull / pairs_all
    dlogits_pair = probs * (dprobs - jnp.sum(probs * dprobs, axis=1, keepdims=True))

    head_f = lax.optimization_barrier(head_t.astype(F32))
    dpooled_pair = jnp.dot(dlogits_pair, head_f, precision=HIGHEST)
    mixed = jnp.dot(probs, head_f, precision=HIGHEST)
    pair_rows = jnp.sum(slope_sums * dpooled_pair, axis=1)
    mass_rows = head_f[:, None] * jnp.einsum("bj,sbc->jsc", probs, slope_sums, precision=HIGHEST)
    mass_rows = mass_rows - jnp.einsum("bj,sbc->jsc", probs, slope_sums * mixed, precision=HIGHEST)
    gram = jnp.einsum("bj,bk->jk", probs, probs, precision=HIGHEST)
    scalars = jnp.concatenate(
        [
            gram.reshape(-1),
            jnp.sum(probs, axis=0),
            jnp.sum(dlogits_pair, axis=0),
            0.5 * jnp.sum(jnp.log(similar))[None],
        ]
    )
    scalars = jnp.pad(scalars, (0, 2 * width - scalars.shape[0]))
    sums = sum_images(
        jnp.concatenate(
            [pair_rows, mass_rows.reshape(3 * classes, -1), scalars[None]], axis=0
        )
    )
    scalars = sums[3 + 3 * classes]
    gram = scalars[: classes * classes].reshape(classes, classes)
    mass_total = scalars[classes * classes : classes * (classes + 1)]
    mass = mass_total / images_all
    pull_mass = ENTROPY_WEIGHT * (jnp.log(mass) + 1.0) / images_all
    pair_total = scalars[classes * (classes + 2)]
    loss = -pair_total / pairs_all + ENTROPY_WEIGHT * jnp.sum(mass * jnp.log(mass))
    grad_bias = (
        scalars[classes * (classes + 1) : classes * (classes + 2)]
        + pull_mass * mass_total
        - jnp.sum(gram * pull_mass[:, None], axis=0)
    )
    upper = sums[:3] + jnp.sum(
        pull_mass[:, None, None] * sums[3 : 3 + 3 * classes].reshape(classes, 3, -1), axis=0
    )
    sum_top, cross_two, cross_short = upper[0], upper[1], upper[2]
    dlogits = dlogits_pair + probs * (
        pull_mass - jnp.sum(probs * pull_mass, axis=1, keepdims=True)
    )
    dlogits_bf = dlogits.astype(BF16)
    grad_head = jnp.einsum("bk,bc->kc", dlogits_bf, pooled, preferred_element_type=F32)
    dpooled = jnp.dot(dlogits, head_f, precision=HIGHEST)
    djoined = (dpooled / 16.0) * slope
    dconv_two = norm_back(
        djoined, centred_two, scale_two, params[2], sum_top, cross_two, pixels
    ).astype(BF16)
    dshort = norm_back(
        djoined, centred_short, scale_short, params[4], sum_top, cross_short, pixels
    ).astype(BF16)

    bits = batch_bits()
    turns = len(bits)

    dhidden_other = conv_back(dconv_two, two_other).astype(BF16)
    dhidden_got = swap(dhidden_other, "chan", 2)
    dhidden = conv_back(dconv_two, two_own)

    centre = in_order(high, likely_mean(params[:2]), likely_mean(params_other), 0)
    pixel_sums = jnp.sum(dconv_two.astype(F32), axis=2)
    tap_sums = jnp.stack(
        [
            jnp.sum(pixel_sums[max(0, 1 - i) : 5 - i, max(0, 1 - j) : 5 - j], axis=(0, 1))
            for i in range(3)
            for j in range(3)
        ]
    )
    grads_two = after(dconv_two, dhidden_other)
    own = weight_grad(hidden, grads_two, 1).reshape(9, 1, 2 * width, -1)
    other = weight_grad(hidden_other, grads_two, 1).reshape(9, 1, 2 * width, -1)
    grad_two = in_order(high, own, other, 1).reshape(-1, 2 * width)
    grad_two = grad_two - outer_taps(centre, tap_sums)
    grad_proj = jnp.einsum("hwbc,hwbk->ck", strided, dshort, preferred_element_type=F32)
    full = jnp.concatenate([grad_two, grad_proj], axis=0)
    keep = lax.dynamic_slice_in_dim(full, low * width, width, 1)
    give = lax.dynamic_slice_in_dim(full, (1 - low) * width, width, 1).astype(BF16)
    dhidden_got, keep, give = lax.optimization_barrier((dhidden_got, keep, give))
    grad_upper = keep + swap(give, "chan", 1).astype(F32)

    def channel_half(full):
        keep = lax.dynamic_slice_in_dim(full, low * width, width, 1)
        give = lax.dynamic_slice_in_dim(full, (1 - low) * width, width, 1)
        return keep + swap(give.astype(BF16), "chan", 1).astype(F32)

    upper = scatter_step(grad_upper, bits[0])
    dhidden = dhidden + dhidden_got.astype(F32)
    dnormed_one = dhidden * silu_slope(normed_one)
    sums = jnp.concatenate(
            [
                jnp.stack([channel_sums(dnormed_one), channel_sums(dnormed_one * centred_one)]),
                grad_head,
                tap_sums,
            ],
            axis=0,
        )
    sums = sum_images(sums)
    sum_low, cross_low = sums[0], sums[1]
    grad_head = lax.dynamic_slice_in_dim(sums[2 : 2 + classes], low * width, width, 1).T
    tap_sums = lax.dynamic_slice_in_dim(sums[2 + classes :], low * width, width, 1)
    missing = outer_taps(centre, tap_sums)
    missing = jnp.concatenate([missing, jnp.zeros(w_proj.shape, F32)], axis=0)
    dnormed_one = after(dnormed_one, upper)
    dconv_one = norm_back(
        dnormed_one, centred_one, scale_one, params[0], sum_low, cross_low, pixels
    ).astype(BF16)
    grad_lower = channel_half(weight_grad(inputs, dconv_one, 2))

    upper = scatter_step(upper, bits[1])
    lower = after(grad_lower, upper)
    for bit in bits[2:]:
        upper = scatter_step(upper, bit)
    upper = upper + own_rows(missing, bits)
    upper_bf = upper.astype(BF16)
    lower_bits = bits[1:] + bits[:1]
    for turn in range(turns):
        lower = scatter_step(lower, lower_bits[turn])
        upper_bf = gather_step(upper_bf, bits[turns - 1 - turn])
    squares = jnp.sum(upper * upper) + jnp.sum(lower * lower)
    grad_norm_params = jnp.stack(
        [cross_low, sum_low, cross_two, sum_top, cross_short, sum_top], axis=0
    )
    grad_norm_params = lax.dynamic_slice_in_dim(grad_norm_params, low * width, width, 1)
    replicated = jnp.sum(grad_norm_params * grad_norm_params) + jnp.sum(grad_head * grad_head)
    replicated = replicated + jnp.sum(grad_bias * grad_bias) / lax.axis_size("chan")
    squares = jnp.broadcast_to(squares + replicated / groups, (8, width))
    bit = 1
    while bit < lax.axis_size("chan"):
        squares = squares + swap(squares, "chan", bit)
        bit *= 2
    lower_bf = lower.astype(BF16)
    for turn in range(turns):
        upper_half = squares.astype(BF16)
        upper_half = lax.optimization_barrier(upper_half)
        lower_half = (squares - upper_half.astype(F32)).astype(BF16)
        split = jnp.concatenate([upper_half, lower_half], axis=0)
        bit = lower_bits[turns - 1 - turn]
        got = swap(jnp.concatenate([lower_bf, split], axis=0), "batch", bit)
        rows = lower_bf.shape[0]
        lower_bf = in_order((lax.axis_index("batch") // bit) % 2, lower_bf, got[:rows], 0)
        squares = squares_of(split) + squares_of(got[rows:])
    grad_upper = upper_bf.astype(F32)
    grad_one = lower_bf.astype(F32)
    grad_two, grad_proj = grad_upper[: w_two.shape[0]], grad_upper[w_two.shape[0] :]

    grad_norm = jnp.sqrt(squares[0, 0])
    scale = jnp.minimum(1.0, CLIP_LIMIT / (grad_norm + 1e-06))
    step = jnp.float32(STEPS)
    bias_one = 1.0 - jnp.power(jnp.float32(BETA_FIRST), step)
    bias_two = 1.0 - jnp.power(jnp.float32(BETA_SECOND), step)
    grads = (grad_one, grad_two, grad_proj, grad_head, grad_bias, grad_norm_params)
    weights = (w_one, w_two, w_proj, head, head_bias, norm_params)
    firsts = (m_one, m_two, m_proj, m_head, m_bias, m_norm)
    seconds = (v_one, v_two, v_proj, v_head, v_bias, v_norm)
    decays = (WEIGHT_DECAY, WEIGHT_DECAY, WEIGHT_DECAY, WEIGHT_DECAY, 0.0, 0.0)
    results = [
        adam(weight, gradient * scale, first, second, bias_one, bias_two, decay)
        for weight, gradient, first, second, decay in zip(weights, grads, firsts, seconds, decays)
    ]
    return (
        loss.reshape(1),
        grad_norm.reshape(1),
        *(result[0] for result in results),
        *(result[1] for result in results),
        *(result[2] for result in results),
    )


def squares_of(split):
    return split[:8].astype(F32) + split[8:].astype(F32)


def own_rows(full, order):
    rows, start = full.shape[0], 0
    for bit in order:
        rows //= 2
        start = start + (lax.axis_index("batch") // bit) % 2 * rows
    return lax.dynamic_slice_in_dim(full, start, rows, 0)


def solution(mesh):
    placed = (
        P("batch", None, None, None),
        P("batch"),
        P("batch", None),
        P(None, "chan"),
        P(None, "chan"),
        P(None, "chan"),
        P("chan", None),
        P(),
        P(None, "chan"),
        P(None, "chan"),
        P(None, "chan"),
        P(None, "chan"),
        P("chan", None),
        P(),
        P(None, "chan"),
        P(None, "chan"),
        P(None, "chan"),
        P(None, "chan"),
        P("chan", None),
        P(),
        P(None, "chan"),
    )
    return jax.shard_map(
        per_device,
        mesh=mesh,
        in_specs=placed,
        out_specs=(
            P(),
            P(),
            P(None, "chan"),
            P(None, "chan"),
            P(None, "chan"),
            P("chan", None),
            P(),
            P(None, "chan"),
            P(None, "chan"),
            P(None, "chan"),
            P(None, "chan"),
            P("chan", None),
            P(),
            P(None, "chan"),
            P(None, "chan"),
            P(None, "chan"),
            P(None, "chan"),
            P("chan", None),
            P(),
            P(None, "chan"),
        ),
        check_vma=False,
    )
```

```python
import math

import jax
import jax.numpy as jnp
from jax import lax
from jax.sharding import PartitionSpec as P

STEPS = 10


NORM_EPS = 1e-05
ENTROPY_WEIGHT = 5.0
CLIP_LIMIT = 0.01
LEARN_RATE = 0.15
BETA_FIRST = 0.9
BETA_SECOND = 0.999
ADAM_EPS = 1e-08
WEIGHT_DECAY = 0.01
MAPS = ("HWNC", "HWIO", "HWNC")
BF16 = jnp.bfloat16
F32 = jnp.float32
HIGHEST = lax.Precision.HIGHEST


def swap(values, axis, bit):
    count = lax.axis_size(axis)
    return lax.ppermute(values, axis, [(i, i ^ bit) for i in range(count)])


def in_order(bit, own, other, axis):
    first = jnp.where(bit == 0, own, other)
    second = jnp.where(bit == 0, other, own)
    return jnp.concatenate([first, second], axis=axis)


def sum_images(values):
    values = values + swap(values, "chan", 1)
    groups = lax.axis_size("batch")
    spread = jnp.broadcast_to(values[None], (groups,) + values.shape)
    return jnp.sum(lax.all_to_all(spread, "batch", 0, 0), axis=0)


def after(values, *others):
    return lax.optimization_barrier((values,) + others)[0]


def sum_images_by_half(values, low):
    columns = values.shape[1] // 2
    give = lax.dynamic_slice_in_dim(values, (1 - low) * columns, columns, 1)
    part = lax.dynamic_slice_in_dim(values, low * columns, columns, 1) + swap(give, "chan", 1)
    groups = lax.axis_size("batch")
    spread = jnp.broadcast_to(part[None], (groups,) + part.shape)
    part = jnp.sum(lax.all_to_all(spread, "batch", 0, 0), axis=0)
    return in_order(low, part, swap(part, "chan", 1), 1)


def batch_bits():
    bits = []
    bit = 1
    while bit < lax.axis_size("batch"):
        bits.append(bit)
        bit *= 2
    return bits


def scatter_step(part, bit):
    rows = part.shape[0] // 2
    mine = (lax.axis_index("batch") // bit) % 2
    keep = lax.dynamic_slice_in_dim(part, mine * rows, rows, 0)
    give = lax.dynamic_slice_in_dim(part, (1 - mine) * rows, rows, 0)
    got = swap(give.astype(BF16), "batch", bit)
    return keep + got.astype(F32)


def gather_step(part, bit):
    mine = (lax.axis_index("batch") // bit) % 2
    got = swap(part, "batch", bit)
    return in_order(mine, part, got, 0)


def conv(maps, weight, stride):
    kernel = weight.reshape(3, 3, weight.shape[0] // 9, weight.shape[1])
    return lax.conv_general_dilated(
        maps,
        kernel,
        (stride, stride),
        ((1, 1), (1, 1)),
        dimension_numbers=MAPS,
        preferred_element_type=F32,
    )


def conv_back(grads, weight):
    kernel = weight.reshape((3, 3) + weight.shape[1:])[::-1, ::-1]
    return lax.conv_general_dilated(
        grads,
        kernel,
        (1, 1),
        ((1, 1), (1, 1)),
        dimension_numbers=("HWNC", "HWOI", "HWNC"),
        preferred_element_type=F32,
    )


def weight_grad(maps, grads, stride):
    result = lax.conv_general_dilated(
        maps,
        grads,
        (1, 1),
        ((1, 2 - stride), (1, 2 - stride)),
        rhs_dilation=(stride, stride),
        dimension_numbers=("HWCN", "HWIO", "HWNC"),
        preferred_element_type=F32,
    )
    return result.reshape(9 * maps.shape[3], grads.shape[3])


def likely_mean(gain_shift):
    gain, shift = gain_shift[0], gain_shift[1]
    spread = math.sqrt(3.0) * gain
    ends = jax.nn.silu(shift + spread) + jax.nn.silu(shift - spread)
    return (4.0 * jax.nn.silu(shift) + ends) / 6.0


def outer_taps(centre, tap_sums):
    return (centre[None, :, None] * tap_sums[:, None, :]).reshape(-1, tap_sums.shape[1])


def channel_sums(values):
    return jnp.sum(values, axis=(0, 1, 2))


def silu_slope(values):
    sigma = jax.nn.sigmoid(values)
    return sigma * (1.0 + values * (1.0 - sigma))


def normalize(values, total, squares, count, gain, shift):
    average = total / count
    spread = squares / count - average * average
    scale = lax.rsqrt(spread + NORM_EPS)
    centred = (values - average) * scale
    return (centred, scale, centred * gain + shift)


def norm_back(grads, centred, scale, gain, sum_grad, sum_cross, count):
    return scale * gain * (grads - sum_grad / count - centred * sum_cross / count)


def adam(weight, gradient, first, second, bias_one, bias_two, decay):
    first_new = BETA_FIRST * first + (1.0 - BETA_FIRST) * gradient
    second_new = BETA_SECOND * second + (1.0 - BETA_SECOND) * gradient * gradient
    stepped = first_new / bias_one / (jnp.sqrt(second_new / bias_two) + ADAM_EPS)
    return (weight - LEARN_RATE * (stepped + decay * weight), first_new, second_new)


def per_device(
    images,
    picks,
    pairs,
    w_one,
    w_two,
    w_proj,
    head,
    head_bias,
    norm_params,
    m_one,
    m_two,
    m_proj,
    m_head,
    m_bias,
    m_norm,
    v_one,
    v_two,
    v_proj,
    v_head,
    v_bias,
    v_norm,
):
    groups = lax.axis_size("batch")
    images_all = picks.shape[0] * groups
    pixels = images_all * 16.0
    pairs_all = pairs.shape[0] * groups
    width = w_one.shape[1]
    classes = head.shape[1]
    chan = lax.axis_index("chan")
    low, high = chan % 2, chan // 2
    count = picks.shape[0] // 2

    one_bf, two_bf, proj_bf = (w.astype(BF16) for w in (w_one, w_two, w_proj))
    one_full = in_order(low, one_bf, swap(one_bf, "chan", 1), 1)
    small = jnp.concatenate([norm_params, head.T], axis=0)
    small = in_order(low, small, swap(small, "chan", 1), 1)
    params = small[:6]
    params_other = swap(params[:2], "chan", 2)
    head_t = small[6:].astype(BF16)
    proj_full = in_order(low, proj_bf, swap(proj_bf, "chan", 1), 1)
    two_full = in_order(low, two_bf, swap(two_bf, "chan", 1), 1)
    two_full = two_full.reshape(9, 2, 2 * width, 2 * width)
    two_own = lax.dynamic_index_in_dim(two_full, high, 1, False)
    two_other = lax.dynamic_index_in_dim(two_full, 1 - high, 1, False)

    mine = lax.dynamic_slice_in_dim(picks, low * count, count, 0)
    inputs = images[mine].transpose(1, 2, 0, 3)
    strided = inputs[::2, ::2]
    one_full, params_other = lax.optimization_barrier((one_full, params_other))
    conv_one = conv(inputs, one_full, 2)
    shortcut = jnp.einsum("hwbc,ck->hwbk", strided, proj_full, preferred_element_type=F32)
    sums = sum_images(
        jnp.stack(
            [
                channel_sums(conv_one),
                channel_sums(conv_one * conv_one),
                channel_sums(shortcut),
                channel_sums(shortcut * shortcut),
            ]
        )
    )
    centred_one, scale_one, normed_one = normalize(
        conv_one, sums[0], sums[1], pixels, params[0], params[1]
    )
    centred_short, scale_short, normed_short = normalize(
        shortcut, sums[2], sums[3], pixels, params[4], params[5]
    )
    hidden = jax.nn.silu(normed_one).astype(BF16)
    hidden_other = swap(hidden, "chan", 2)
    conv_two = conv(hidden, two_own.reshape(-1, 2 * width), 1)
    conv_two = conv_two + conv(hidden_other, two_other.reshape(-1, 2 * width), 1)
    sums = sum_images(jnp.stack([channel_sums(conv_two), channel_sums(conv_two * conv_two)]))
    centred_two, scale_two, normed_two = normalize(
        conv_two, sums[0], sums[1], pixels, params[2], params[3]
    )
    summed = normed_two + normed_short
    joined = jax.nn.silu(summed)
    slope = silu_slope(summed)
    pooled = (jnp.sum(joined, axis=(0, 1)) / 16.0).astype(BF16)
    slope_sums = jnp.stack(
        [
            jnp.sum(slope, axis=(0, 1)),
            jnp.sum(slope * centred_two, axis=(0, 1)),
            jnp.sum(slope * centred_short, axis=(0, 1)),
        ]
    ) / 16.0

    logits_part = jnp.einsum("bc,kc->bk", pooled, head_t, preferred_element_type=F32)
    logits_part = in_order(low, logits_part, swap(logits_part, "chan", 1), 0)
    logits = logits_part + swap(logits_part, "chan", 2) + head_bias
    probs_all = jax.nn.softmax(logits, axis=1)
    probs = lax.dynamic_slice_in_dim(probs_all, low * count, count, 0)
    ids = jnp.arange(2 * count, dtype=pairs.dtype)
    hot_a = (pairs[:, :1] == ids).astype(F32)
    hot_b = (pairs[:, 1:] == ids).astype(F32)
    probs_a = jnp.dot(hot_a, probs_all, precision=HIGHEST)
    probs_b = jnp.dot(hot_b, probs_all, precision=HIGHEST)
    similar = jnp.sum(probs_a * probs_b, axis=1, keepdims=True)
    pull = jnp.einsum("pb,pk->bk", hot_a, probs_b / similar, precision=HIGHEST)
    pull = pull + jnp.einsum("pb,pk->bk", hot_b, probs_a / similar, precision=HIGHEST)
    pull = lax.dynamic_slice_in_dim(pull, low * count, count, 0)
    dprobs = -pull / pairs_all
    dlogits_pair = probs * (dprobs - jnp.sum(probs * dprobs, axis=1, keepdims=True))

    head_f = lax.optimization_barrier(head_t.astype(F32))
    dpooled_pair = jnp.dot(dlogits_pair, head_f, precision=HIGHEST)
    mixed = jnp.dot(probs, head_f, precision=HIGHEST)
    pair_rows = jnp.sum(slope_sums * dpooled_pair, axis=1)
    mass_rows = head_f[:, None] * jnp.einsum("bj,sbc->jsc", probs, slope_sums, precision=HIGHEST)
    mass_rows = mass_rows - jnp.einsum("bj,sbc->jsc", probs, slope_sums * mixed, precision=HIGHEST)
    gram = jnp.einsum("bj,bk->jk", probs, probs, precision=HIGHEST)
    scalars = jnp.concatenate(
        [
            gram.reshape(-1),
            jnp.sum(probs, axis=0),
            jnp.sum(dlogits_pair, axis=0),
            0.5 * jnp.sum(jnp.log(similar))[None],
        ]
    )
    scalars = jnp.pad(scalars, (0, 2 * width - scalars.shape[0]))
    sums = sum_images_by_half(
        jnp.concatenate(
            [pair_rows, mass_rows.reshape(3 * classes, -1), scalars[None]], axis=0
        ),
        low,
    )
    scalars = sums[3 + 3 * classes]
    gram = scalars[: classes * classes].reshape(classes, classes)
    mass_total = scalars[classes * classes : classes * (classes + 1)]
    mass = mass_total / images_all
    pull_mass = ENTROPY_WEIGHT * (jnp.log(mass) + 1.0) / images_all
    pair_total = scalars[classes * (classes + 2)]
    loss = -pair_total / pairs_all + ENTROPY_WEIGHT * jnp.sum(mass * jnp.log(mass))
    grad_bias = (
        scalars[classes * (classes + 1) : classes * (classes + 2)]
        + pull_mass * mass_total
        - jnp.sum(gram * pull_mass[:, None], axis=0)
    )
    upper = sums[:3] + jnp.sum(
        pull_mass[:, None, None] * sums[3 : 3 + 3 * classes].reshape(classes, 3, -1), axis=0
    )
    sum_top, cross_two, cross_short = upper[0], upper[1], upper[2]
    dlogits = dlogits_pair + probs * (
        pull_mass - jnp.sum(probs * pull_mass, axis=1, keepdims=True)
    )
    dlogits_bf = dlogits.astype(BF16)
    grad_head = jnp.einsum("bk,bc->kc", dlogits_bf, pooled, preferred_element_type=F32)
    dpooled = jnp.dot(dlogits, head_f, precision=HIGHEST)
    djoined = (dpooled / 16.0) * slope
    dconv_two = norm_back(
        djoined, centred_two, scale_two, params[2], sum_top, cross_two, pixels
    ).astype(BF16)
    dshort = norm_back(
        djoined, centred_short, scale_short, params[4], sum_top, cross_short, pixels
    ).astype(BF16)

    bits = batch_bits()
    turns = len(bits)

    dhidden_other = conv_back(dconv_two, two_other).astype(BF16)
    dhidden_got = swap(dhidden_other, "chan", 2)
    dhidden = conv_back(dconv_two, two_own)

    centre = in_order(high, likely_mean(params[:2]), likely_mean(params_other), 0)
    pixel_sums = jnp.sum(dconv_two.astype(F32), axis=2)
    tap_sums = jnp.stack(
        [
            jnp.sum(pixel_sums[max(0, 1 - i) : 5 - i, max(0, 1 - j) : 5 - j], axis=(0, 1))
            for i in range(3)
            for j in range(3)
        ]
    )
    grads_two = after(dconv_two, dhidden_other)
    own = weight_grad(hidden, grads_two, 1).reshape(9, 1, 2 * width, -1)
    other = weight_grad(hidden_other, grads_two, 1).reshape(9, 1, 2 * width, -1)
    grad_two = in_order(high, own, other, 1).reshape(-1, 2 * width)
    grad_two = grad_two - outer_taps(centre, tap_sums)
    grad_proj = jnp.einsum("hwbc,hwbk->ck", strided, dshort, preferred_element_type=F32)
    full = jnp.concatenate([grad_two, grad_proj], axis=0)
    keep = lax.dynamic_slice_in_dim(full, low * width, width, 1)
    give = lax.dynamic_slice_in_dim(full, (1 - low) * width, width, 1).astype(BF16)
    dhidden_got, keep, give = lax.optimization_barrier((dhidden_got, keep, give))
    grad_upper = keep + swap(give, "chan", 1).astype(F32)

    def channel_half(full):
        keep = lax.dynamic_slice_in_dim(full, low * width, width, 1)
        give = lax.dynamic_slice_in_dim(full, (1 - low) * width, width, 1)
        return keep + swap(give.astype(BF16), "chan", 1).astype(F32)

    upper = scatter_step(grad_upper, bits[0])
    dhidden = dhidden + dhidden_got.astype(F32)
    dnormed_one = dhidden * silu_slope(normed_one)
    sums = jnp.concatenate(
            [
                jnp.stack([channel_sums(dnormed_one), channel_sums(dnormed_one * centred_one)]),
                grad_head,
                tap_sums,
            ],
            axis=0,
        )
    sums = sum_images(sums)
    sum_low, cross_low = sums[0], sums[1]
    grad_head = lax.dynamic_slice_in_dim(sums[2 : 2 + classes], low * width, width, 1).T
    tap_sums = lax.dynamic_slice_in_dim(sums[2 + classes :], low * width, width, 1)
    missing = outer_taps(centre, tap_sums)
    missing = jnp.concatenate([missing, jnp.zeros(w_proj.shape, F32)], axis=0)
    dnormed_one = after(dnormed_one, upper)
    dconv_one = norm_back(
        dnormed_one, centred_one, scale_one, params[0], sum_low, cross_low, pixels
    ).astype(BF16)
    grad_lower = channel_half(weight_grad(inputs, dconv_one, 2))

    upper = scatter_step(upper, bits[1])
    lower = after(grad_lower, upper)
    for bit in bits[2:]:
        upper = scatter_step(upper, bit)
    upper = upper + own_rows(missing, bits)
    upper_bf = upper.astype(BF16)
    lower_bits = bits[1:] + bits[:1]
    for turn in range(turns):
        lower = scatter_step(lower, lower_bits[turn])
        upper_bf = gather_step(upper_bf, bits[turns - 1 - turn])
    squares = jnp.sum(upper * upper) + jnp.sum(lower * lower)
    grad_norm_params = jnp.stack(
        [cross_low, sum_low, cross_two, sum_top, cross_short, sum_top], axis=0
    )
    grad_norm_params = lax.dynamic_slice_in_dim(grad_norm_params, low * width, width, 1)
    replicated = jnp.sum(grad_norm_params * grad_norm_params) + jnp.sum(grad_head * grad_head)
    replicated = replicated + jnp.sum(grad_bias * grad_bias) / lax.axis_size("chan")
    squares = jnp.broadcast_to(squares + replicated / groups, (8, width))
    bit = 1
    while bit < lax.axis_size("chan"):
        squares = squares + swap(squares, "chan", bit)
        bit *= 2
    lower_bf = lower.astype(BF16)
    for turn in range(turns):
        upper_half = squares.astype(BF16)
        upper_half = lax.optimization_barrier(upper_half)
        lower_half = (squares - upper_half.astype(F32)).astype(BF16)
        split = jnp.concatenate([upper_half, lower_half], axis=0)
        bit = lower_bits[turns - 1 - turn]
        got = swap(jnp.concatenate([lower_bf, split], axis=0), "batch", bit)
        rows = lower_bf.shape[0]
        lower_bf = in_order((lax.axis_index("batch") // bit) % 2, lower_bf, got[:rows], 0)
        squares = squares_of(split) + squares_of(got[rows:])
    grad_upper = upper_bf.astype(F32)
    grad_one = lower_bf.astype(F32)
    grad_two, grad_proj = grad_upper[: w_two.shape[0]], grad_upper[w_two.shape[0] :]

    grad_norm = jnp.sqrt(squares[0, 0])
    scale = jnp.minimum(1.0, CLIP_LIMIT / (grad_norm + 1e-06))
    step = jnp.float32(STEPS)
    bias_one = 1.0 - jnp.power(jnp.float32(BETA_FIRST), step)
    bias_two = 1.0 - jnp.power(jnp.float32(BETA_SECOND), step)
    grads = (grad_one, grad_two, grad_proj, grad_head, grad_bias, grad_norm_params)
    weights = (w_one, w_two, w_proj, head, head_bias, norm_params)
    firsts = (m_one, m_two, m_proj, m_head, m_bias, m_norm)
    seconds = (v_one, v_two, v_proj, v_head, v_bias, v_norm)
    decays = (WEIGHT_DECAY, WEIGHT_DECAY, WEIGHT_DECAY, WEIGHT_DECAY, 0.0, 0.0)
    results = [
        adam(weight, gradient * scale, first, second, bias_one, bias_two, decay)
        for weight, gradient, first, second, decay in zip(weights, grads, firsts, seconds, decays)
    ]
    return (
        loss.reshape(1),
        grad_norm.reshape(1),
        *(result[0] for result in results),
        *(result[1] for result in results),
        *(result[2] for result in results),
    )


def squares_of(split):
    return split[:8].astype(F32) + split[8:].astype(F32)


def own_rows(full, order):
    rows, start = full.shape[0], 0
    for bit in order:
        rows //= 2
        start = start + (lax.axis_index("batch") // bit) % 2 * rows
    return lax.dynamic_slice_in_dim(full, start, rows, 0)


def solution(mesh):
    placed = (
        P("batch", None, None, None),
        P("batch"),
        P("batch", None),
        P(None, "chan"),
        P(None, "chan"),
        P(None, "chan"),
        P("chan", None),
        P(),
        P(None, "chan"),
        P(None, "chan"),
        P(None, "chan"),
        P(None, "chan"),
        P("chan", None),
        P(),
        P(None, "chan"),
        P(None, "chan"),
        P(None, "chan"),
        P(None, "chan"),
        P("chan", None),
        P(),
        P(None, "chan"),
    )
    return jax.shard_map(
        per_device,
        mesh=mesh,
        in_specs=placed,
        out_specs=(
            P(),
            P(),
            P(None, "chan"),
            P(None, "chan"),
            P(None, "chan"),
            P("chan", None),
            P(),
            P(None, "chan"),
            P(None, "chan"),
            P(None, "chan"),
            P(None, "chan"),
            P("chan", None),
            P(),
            P(None, "chan"),
            P(None, "chan"),
            P(None, "chan"),
            P(None, "chan"),
            P("chan", None),
            P(),
            P(None, "chan"),
        ),
        check_vma=False,
    )
```
